32 devices in a mesh: dp: 16 (over z, y, x), query: 2 (over core).
Axes of the slice: x: 2, y: 2, z: 4, core: 2. Of those that a mesh axis runs over, the one named last changes fastest.
Arguments:
- hidden_acts: bfloat16 [2048, 4, 14336], P(('dp', 'query')), may hold values from -5 to 5
- out_grads: bfloat16 [2048, 4, 4096], P(('dp', 'query')), may hold values from -5 to 5
- loss_mask: int32 [2048, 4], P(('dp', 'query')), may hold values from 0 to 1, as said below
- proj_in: bfloat16 [32, 14336], replicated, may hold values from -0.046875 to 0.046875
- proj_out: bfloat16 [32, 4096], replicated, may hold values from -0.09375 to 0.09375
- queries: float32 [256, 1024], P('query'), may hold values from -0.3125 to 0.3125
Outputs:
- scores: float32 [2048, 256], P(('dp', 'query'))
The draws below stay inside these ranges and needn't reach their ends.
Inputs may be any that keep to these rules, and one draw needn't show every extreme that they name: `loss_mask`: the first token of every sequence counts.
All inputs are finite; a program needn't handle non-finite values.
Results may differ from the reference program's by a relative error of at most 0.0007.
Values sent between devices are 32-bit elements; how exact they have to be, the bound alone decides.
A program may use at most 128 MiB of HBM per device.

```python
import jax
import jax.numpy as jnp
from jax import lax

D = 4096
FF = 14336
P_IN = 32
P_OUT = 32
K = 1024
SEQ_LEN = 4
QUERIES = 256
SEQS = 2048


def draw_loss_mask(key, part):
    position = jnp.arange(SEQS, dtype=jnp.int32)
    live_level = 300 + 600 * position // SEQS
    drawn_ints = jax.random.randint(key, (SEQS, SEQ_LEN), 0, 1000, dtype=jnp.int32)
    is_live = (drawn_ints < live_level[:, None]).astype(jnp.int32)
    leading = (jnp.arange(SEQ_LEN, dtype=jnp.int32) == 0)[None, :]
    return jnp.where(leading, 1, is_live).astype(jnp.int32)


def group_count():
    return max(1, P_IN * P_OUT // 16)


def group_labels(base_key):
    return jax.random.randint(jax.random.fold_in(base_key, 101), (SEQS,), 0, group_count(), dtype=jnp.int32)


def grouped_rows(base_key, row_width, salt_value):
    groups = group_count()
    labels = group_labels(base_key)
    side_key = jax.random.fold_in(base_key, salt_value)
    direction_key, mixing_key, ladder_key, jitter_key = jax.random.split(side_key, 4)
    directions = jax.random.normal(direction_key, (groups, 4, row_width), jnp.float32)
    ladder = jax.random.permutation(ladder_key, groups).astype(jnp.float32) / max(groups - 1, 1)
    scales = 0.45 * jnp.exp(ladder * jnp.log(1.6 / 0.45))
    mixing = 0.5 * jax.random.normal(mixing_key, (SEQS, SEQ_LEN, 4), jnp.float32)
    mixing = mixing * scales[labels][:, None, None]
    blocks = 16 if SEQS % 16 == 0 else 1
    block_rows = SEQS // blocks

    def one_block(inputs):
        mixing_part, label_part, position = inputs
        picked = directions[label_part]
        combined = jnp.einsum('stj,sjw->stw', mixing_part, picked)
        part_key = jax.random.fold_in(jitter_key, position)
        jitter = 0.1 * jax.random.normal(part_key, combined.shape, jnp.float32)
        return jnp.clip(combined + jitter, -5.0, 5.0).astype(jnp.bfloat16)
    stacked = lax.map(one_block, (mixing.reshape(blocks, block_rows, SEQ_LEN, 4), labels.reshape(blocks, block_rows), jnp.arange(blocks, dtype=jnp.int32)))
    return stacked.reshape(SEQS, SEQ_LEN, row_width)


def draw_hidden_acts(key, part):
    return grouped_rows(key, FF, 202)


def draw_out_grads(key, part):
    return grouped_rows(key, D, 303)


def steps_of(stream_key, extent, cuts, smallest, largest):
    level = 1.0
    for axis_at, parts in cuts:
        steps = jax.random.uniform(jax.random.fold_in(jax.random.fold_in(stream_key, 6), axis_at), (parts,), jnp.float32, smallest / len(cuts), largest / len(cuts))
        level = level * jnp.repeat(jnp.exp(steps), extent[axis_at] // parts).reshape((-1,) + (1,) * (len(extent) - 1 - axis_at))
    return level


def normal_values(rng, shape, deviation, bound, shards=(), kind=jnp.bfloat16):
    gain = steps_of(rng, shape, shards, -0.22, 0.18) if shards else 1.0
    array = jax.random.normal(rng, shape, jnp.float32) * deviation * gain
    return jnp.minimum(jnp.maximum(array, -bound), bound).astype(kind)


def setup_inputs(seed: int = 0) -> dict:
    streams_of = jax.random.split(jax.random.key(seed), 7)
    return {
        "hidden_acts": draw_hidden_acts(jax.random.fold_in(streams_of[6], 71), 0),
        "out_grads": draw_out_grads(jax.random.fold_in(streams_of[6], 71), 0),
        "loss_mask": draw_loss_mask(jax.random.fold_in(streams_of[6], 71), 0),
        "proj_in": normal_values(streams_of[3], (P_IN, FF), FF ** -0.5, 0.046875),
        "proj_out": normal_values(streams_of[4], (P_OUT, D), D ** -0.5, 0.09375),
        "queries": normal_values(streams_of[5], (QUERIES, K), (0.7 * K ** -0.5), 0.3125, ((0, 2),), jnp.float32),
    }


def damped_solve(factor, columns):
    halfway = jax.scipy.linalg.solve_triangular(factor, columns, lower=True)
    return jax.scipy.linalg.solve_triangular(factor, halfway, lower=True, trans=1)

def reference(hidden_acts, out_grads, loss_mask, proj_in, proj_out, queries):
    is_live = loss_mask.astype(jnp.float32)
    token_total = jnp.sum(is_live)
    act_proj = lax.dot_general(hidden_acts.reshape(-1, FF).astype(jnp.float32), proj_in.astype(jnp.float32), (((1,), (1,)), ((), ())), preferred_element_type=jnp.float32).reshape(SEQS, SEQ_LEN, P_IN)
    grad_proj = lax.dot_general(out_grads.reshape(-1, D).astype(jnp.float32), proj_out.astype(jnp.float32), (((1,), (1,)), ((), ())), preferred_element_type=jnp.float32).reshape(SEQS, SEQ_LEN, P_OUT)
    weighted = grad_proj * is_live[:, :, None]
    outer = jnp.einsum('stg,stx->sgx', weighted, act_proj, precision=lax.Precision.HIGHEST).reshape(SEQS, K)
    sketch = outer / token_total
    fisher = lax.dot_general(sketch, sketch, (((0,), (0,)), ((), ())), precision=lax.Precision.HIGHEST)
    damping = 0.1 * jnp.trace(fisher) / K
    system = fisher + damping * jnp.eye(K, dtype=jnp.float32)
    factor = jnp.linalg.cholesky(system)
    solved = damped_solve(factor, queries.T)
    return jnp.dot(sketch, solved, precision=lax.Precision.HIGHEST)
```

```python
import functools

import jax
import jax.numpy as jnp
from jax import lax
from jax.experimental import pallas as pl
from jax.experimental.pallas import tpu as pltpu
from jax.sharding import PartitionSpec as P

BLOCK = 128
SUB = 8
HIGHEST = lax.Precision.HIGHEST
NN = (((1,), (0,)), ((), ()))
NT = (((1,), (1,)), ((), ()))


def dot(a, b, dims=NN):
    return lax.dot_general(a, b, dims, precision=HIGHEST, preferred_element_type=jnp.float32)


def negated_inverse(block):
    size = block.shape[0]
    tiles = size // SUB
    rows = [block[SUB * t:SUB * (t + 1), :] for t in range(tiles)]
    lane = lax.broadcasted_iota(jnp.int32, (SUB, size), 1)
    sub = lax.broadcasted_iota(jnp.int32, (SUB, size), 0)

    def spread(x, at):
        return jnp.broadcast_to(x[:, at:at + 1], (SUB, size))

    for t in range(tiles):
        first = SUB * t
        inside = (lane >= first) & (lane < first + SUB)
        columns = [spread(rows[t], first + i) for i in range(SUB)]
        panel = jnp.where(inside, jnp.where(lane - first == sub, -1.0, 0.0), rows[t])
        for i in range(SUB):
            pivot = jnp.broadcast_to(columns[i][i:i + 1, :], (SUB, size))
            inverse = 1.0 / pivot
            at_pivot = sub == i

            def eliminate(x):
                scaled = jnp.broadcast_to(x[i:i + 1, :], (SUB, size)) * inverse
                return jnp.where(at_pivot, scaled, x - columns[i] * scaled)

            panel = eliminate(panel)
            for j in range(i + 1, SUB):
                columns[j] = eliminate(columns[j])
        spread_panel = [jnp.broadcast_to(panel[i:i + 1, :], (SUB, size)) for i in range(SUB)]
        updated = []
        for u in range(tiles):
            if u == t:
                updated.append(panel)
                continue
            terms = [spread(rows[u], first + i) * spread_panel[i] for i in range(SUB)]
            while len(terms) > 1:
                terms = [terms[i] + terms[i + 1] for i in range(0, len(terms), 2)]
            updated.append(jnp.where(inside, 0.0, rows[u]) - terms[0])
        rows = updated
    return jnp.concatenate(rows, axis=0)


def solve_kernel(fisher_ref, sketch_ref, queries_ref, scores_ref, work, solved):
    width = fisher_ref.shape[0]
    blocks = width // BLOCK
    work[:width, :] = fisher_ref[...]
    work[width:, :] = sketch_ref[...]
    diagonal = (lax.broadcasted_iota(jnp.int32, (BLOCK, BLOCK), 0)
                == lax.broadcasted_iota(jnp.int32, (BLOCK, BLOCK), 1))
    spans = [pl.ds(b * BLOCK, BLOCK) for b in range(blocks)]
    kept = jnp.zeros((BLOCK, BLOCK), jnp.float32)
    for span in spans:
        kept = kept + jnp.where(diagonal, work[span, span], 0.0)
    damping = 0.1 * jnp.sum(kept) / width

    @pl.loop(0, blocks)
    def _(k):
        start = pl.multiple_of(k * BLOCK, BLOCK)
        here = pl.ds(start, BLOCK)
        block = work[here, here]
        inverse = -negated_inverse(jnp.where(diagonal, block + damping, block))
        for b in range(blocks):
            @pl.when(k == b)
            def _():
                below = (b + 1) * BLOCK
                panel = work[below:, spans[b]]
                scaled = dot(panel, inverse)
                work[below:, spans[b]] = scaled
                for left in range(below, width, 2 * BLOCK):
                    right = min(left + 2 * BLOCK, width)
                    work[left:, left:right] -= dot(
                        scaled[left - below:, :], panel[left - below:right - below, :], NT)

    solved[:, spans[-1]] = work[width:, spans[-1]]
    for b in range(blocks - 2, -1, -1):
        above = (b + 1) * BLOCK
        solved[:, spans[b]] = work[width:, spans[b]] - dot(
            solved[:, above:], work[above:width, spans[b]])
    scores_ref[...] = dot(solved[...], queries_ref[...], NT)


def solve_scores(fisher, sketch, queries):
    width = fisher.shape[0]
    rows = sketch.shape[0]
    whole = pl.BlockSpec(memory_space=pltpu.VMEM)
    return pl.pallas_call(
        solve_kernel,
        out_shape=jax.ShapeDtypeStruct((rows, queries.shape[0]), jnp.float32),
        in_specs=[whole] * 3,
        out_specs=whole,
        scratch_shapes=[
            pltpu.VMEM((width + rows, width), jnp.float32),
            pltpu.VMEM((rows, width), jnp.float32),
        ],
        compiler_params=pltpu.CompilerParams(vmem_limit_bytes=48 * 2**20),
        name="solve_scores",
    )(fisher, sketch, queries)


def on_device(axes, hidden_acts, out_grads, loss_mask, proj_in, proj_out, queries):
    seq_count, seq_tokens, hidden_width = hidden_acts.shape
    model_width = out_grads.shape[2]
    gathered = lax.all_gather(queries, "query", axis=0, tiled=True)
    is_live = loss_mask.astype(jnp.float32)
    local_count = jnp.sum(is_live)
    act_proj = lax.dot_general(
        hidden_acts.reshape(-1, hidden_width),
        proj_in,
        (((1,), (1,)), ((), ())),
        preferred_element_type=jnp.float32,
    ).reshape(seq_count, seq_tokens, proj_in.shape[0])
    grad_proj = lax.dot_general(
        out_grads.reshape(-1, model_width),
        proj_out,
        (((1,), (1,)), ((), ())),
        preferred_element_type=jnp.float32,
    ).reshape(seq_count, seq_tokens, proj_out.shape[0])
    weighted = grad_proj * is_live[:, :, None]
    outer = jnp.einsum("stg,stx->sgx", weighted, act_proj, precision=HIGHEST).reshape(
        seq_count, -1
    )
    token_total = lax.psum(local_count, axes)
    sketch = outer / token_total
    gram = lax.dot_general(sketch, sketch, (((0,), (0,)), ((), ())), precision=HIGHEST)
    fisher = lax.psum(gram, axes)
    return solve_scores(fisher, sketch, gathered)


def solution(mesh):
    return jax.shard_map(
        functools.partial(on_device, ("dp", "query")),
        mesh=mesh,
        in_specs=(
            P(("dp", "query"), None, None),
            P(("dp", "query"), None, None),
            P(("dp", "query"), None),
            P(),
            P(),
            P("query", None),
        ),
        out_specs=P(("dp", "query"), None),
        check_vma=False,
    )
```

```python
import functools

import jax
import jax.numpy as jnp
from jax import lax
from jax.experimental import pallas as pl
from jax.experimental.pallas import tpu as pltpu
from jax.sharding import PartitionSpec as P

BLOCK = 128
SUB = 8
LANES = 128
TOKENS = 4
MOST_GATHERED = 64
HIGHEST = lax.Precision.HIGHEST
NN = (((1,), (0,)), ((), ()))
NT = (((1,), (1,)), ((), ()))


def dot(a, b, dims=NN, precision=HIGHEST):
    return lax.dot_general(a, b, dims, precision=precision, preferred_element_type=jnp.float32)


def halves_of(x):
    high = x.astype(jnp.bfloat16)
    return high, (x - high.astype(jnp.float32)).astype(jnp.bfloat16)


def three_products(x, y=None):
    x_high, x_low = halves_of(x)
    y_high, y_low = (x_high, x_low) if y is None else halves_of(y)
    return (jnp.concatenate([x_high, x_high, x_low], axis=1),
            jnp.concatenate([y_high, y_low, y_high], axis=1))


def negated_inverse(block):
    size = block.shape[0]
    tiles = size // SUB
    rows = [block[SUB * t:SUB * (t + 1), :] for t in range(tiles)]
    lane = lax.broadcasted_iota(jnp.int32, (SUB, size), 1)
    sub = lax.broadcasted_iota(jnp.int32, (SUB, size), 0)

    def spread(x, at):
        return jnp.broadcast_to(x[:, at:at + 1], (SUB, size))

    for t in range(tiles):
        first = SUB * t
        inside = (lane >= first) & (lane < first + SUB)
        columns = [spread(rows[t], first + i) for i in range(SUB)]
        panel = jnp.where(inside, jnp.where(lane - first == sub, -1.0, 0.0), rows[t])
        for i in range(SUB):
            pivot = jnp.broadcast_to(columns[i][i:i + 1, :], (SUB, size))
            inverse = 1.0 / pivot
            at_pivot = sub == i

            def eliminate(x):
                scaled = jnp.broadcast_to(x[i:i + 1, :], (SUB, size)) * inverse
                return jnp.where(at_pivot, scaled, x - columns[i] * scaled)

            panel = eliminate(panel)
            for j in range(i + 1, SUB):
                columns[j] = eliminate(columns[j])
        spread_panel = [jnp.broadcast_to(panel[i:i + 1, :], (SUB, size)) for i in range(SUB)]
        updated = []
        for u in range(tiles):
            if u == t:
                updated.append(panel)
                continue
            terms = [spread(rows[u], first + i) * spread_panel[i] for i in range(SUB)]
            while len(terms) > 1:
                terms = [terms[i] + terms[i + 1] for i in range(0, len(terms), 2)]
            updated.append(jnp.where(inside, 0.0, rows[u]) - terms[0])
        rows = updated
    return jnp.concatenate(rows, axis=0)


def solve_kernel(fisher_ref, sketch_ref, queries_ref, scores_ref, work, solved):
    width = fisher_ref.shape[0]
    work[:width, :] = fisher_ref[...]
    work[width:, :] = sketch_ref[...]
    eliminate(width, queries_ref, scores_ref, work, solved, 1.0)


def eliminate(width, queries_ref, scores_ref, work, solved, factor):
    blocks = width // BLOCK
    diagonal = (lax.broadcasted_iota(jnp.int32, (BLOCK, BLOCK), 0)
                == lax.broadcasted_iota(jnp.int32, (BLOCK, BLOCK), 1))
    spans = [pl.ds(b * BLOCK, BLOCK) for b in range(blocks)]
    kept = jnp.zeros((BLOCK, BLOCK), jnp.float32)
    for span in spans:
        kept = kept + jnp.where(diagonal, work[span, span], 0.0)
    damping = 0.1 * jnp.sum(kept) / width

    @pl.loop(0, blocks)
    def _(k):
        start = pl.multiple_of(k * BLOCK, BLOCK)
        here = pl.ds(start, BLOCK)
        block = work[here, here]
        inverse = -negated_inverse(jnp.where(diagonal, block + damping, block))
        for b in range(blocks):
            @pl.when(k == b)
            def _():
                below = (b + 1) * BLOCK
                panel = work[below:, spans[b]]
                scaled = dot(panel, inverse)
                work[below:, spans[b]] = scaled
                if below == width:
                    return
                tall, wide = three_products(scaled, panel[:width - below, :])
                for left in range(below, width, 2 * BLOCK):
                    right = min(left + 2 * BLOCK, width)
                    work[left:, left:right] -= dot(
                        tall[left - below:, :], wide[left - below:right - below, :], NT, None)

    solved[:, spans[-1]] = work[width:, spans[-1]]
    for b in range(blocks - 2, -1, -1):
        above = (b + 1) * BLOCK
        solved[:, spans[b]] = work[width:, spans[b]] - dot(
            solved[:, above:], work[above:width, spans[b]])
    scores_ref[...] = dot(solved[...], queries_ref[...], NT) * factor


def solve_scores(fisher, sketch, queries):
    width = fisher.shape[0]
    rows = sketch.shape[0]
    whole = pl.BlockSpec(memory_space=pltpu.VMEM)
    return pl.pallas_call(
        solve_kernel,
        out_shape=jax.ShapeDtypeStruct((rows, queries.shape[0]), jnp.float32),
        in_specs=[whole] * 3,
        out_specs=whole,
        scratch_shapes=[
            pltpu.VMEM((width + rows, width), jnp.float32),
            pltpu.VMEM((rows, width), jnp.float32),
        ],
        compiler_params=pltpu.CompilerParams(vmem_limit_bytes=48 * 2**20),
        name="solve_scores",
    )(fisher, sketch, queries)


NAMES = ("dp", "query")


def gather_kernel(dims, mine_ref, slots_ref, own_sem, send_sem, recv_sem):
    n = len(dims)
    dp, core = lax.axis_index("dp"), lax.axis_index("query")
    bits = [lax.rem(lax.div(dp, d), 2) for d in dims]
    partners = [dp + d - 2 * d * bit for d, bit in zip(dims, bits)]
    everyone = [{"dp": p, "query": core} for p in partners] + [{"dp": dp, "query": 1 - core}]

    barrier = pltpu.get_barrier_semaphore()
    for device in everyone:
        pl.semaphore_signal(barrier, inc=1, device_id=device, device_id_type=pl.DeviceIdType.MESH)
    own = pltpu.make_async_copy(mine_ref, slots_ref.at[(core, *bits)], own_sem)
    own.start()
    own.wait()
    pl.semaphore_wait(barrier, len(everyone))

    count = [0]
    copies = []

    def send(index, device):
        part = slots_ref.at[index]
        at = count[0]
        count[0] += 1
        copy = pltpu.make_async_remote_copy(
            src_ref=part, dst_ref=part, send_sem=send_sem.at[at], recv_sem=recv_sem.at[at],
            device_id=device, device_id_type=pl.DeviceIdType.MESH)
        copy.start()
        copies.append(copy)
        return copy

    def forward(index):
        return send(index, everyone[-1])

    every = slice(None)
    siblings = [forward((core, *bits))]
    held = list(bits)
    for a in range(n - 2):
        send((core, *held), everyone[a]).wait_recv()
        came = list(held)
        came[a] = 1 - bits[a]
        siblings.append(forward((core, *came)))
        held[a] = every
    halves = [(0, (n - 2, n - 1)), (1, (n - 1, n - 2))]
    helds = []
    for half, _ in halves:
        one = list(held)
        one[0] = half
        helds.append(one)
    for turn in range(2):
        flying = [send((core, *helds[h]), everyone[order[turn]]) for h, order in halves]
        for (h, order), copy in zip(halves, flying):
            copy.wait_recv()
            axis = order[turn]
            came = list(helds[h])
            came[axis] = 1 - bits[axis]
            siblings.append(forward((core, *came)))
            helds[h][axis] = every
    for copy in siblings:
        copy.wait_recv()
    for copy in copies:
        copy.wait_send()


def gather_blocks(block, dp_size):
    dims = []
    d = dp_size // 2
    while d:
        dims.append(d)
        d //= 2
    n = len(dims)
    transfers = 2 * (n - 2 + 4) + 1
    anywhere = pl.BlockSpec(memory_space=pl.ANY)
    return pl.pallas_call(
        functools.partial(gather_kernel, tuple(dims)),
        out_shape=jax.ShapeDtypeStruct((2,) + (2,) * n + block.shape, block.dtype),
        in_specs=[anywhere],
        out_specs=anywhere,
        scratch_shapes=[
            pltpu.SemaphoreType.DMA,
            pltpu.SemaphoreType.DMA((transfers,)),
            pltpu.SemaphoreType.DMA((transfers,)),
        ],
        compiler_params=pltpu.CompilerParams(collective_id=0, has_side_effects=True),
        name="gather_tokens",
    )(block)


def pair_sketch(first, second, in_width, out_width):
    lanes = 2 * LANES
    low = lax.broadcasted_iota(jnp.int32, (in_width + out_width, LANES), 1) < LANES // 2
    total = None
    for start in range(0, lanes, LANES):
        one, two = first[:, start:start + LANES], second[:, start:start + LANES]
        for token in (jnp.where(low, one, pltpu.roll(two, LANES // 2, 1)),
                      jnp.where(low, pltpu.roll(one, LANES // 2, 1), two)):
            acts = token[out_width:, :]
            term = [token[g:g + 1, :] * acts for g in range(out_width)]
            total = term if total is None else [t + u for t, u in zip(total, term)]
    return total


def whole_kernel(in_width, out_width, mine_ref, slots_ref, queries_ref, scores_ref,
                 work, solved, sketches):
    width = in_width * out_width
    rows = in_width + out_width
    devices = slots_ref.shape[0]
    per_turn = sketches.shape[1] // (LANES // 2)

    def fill(first, second, column):
        parts = pair_sketch(first, second, in_width, out_width)
        for g, part in enumerate(parts):
            sketches[g * in_width:(g + 1) * in_width, column:column + LANES] = part

    work[:width, :] = jnp.zeros((width, width), jnp.float32)

    @pl.loop(0, devices // per_turn)
    def _(turn):
        for p in range(0, per_turn, 2):
            fill(slots_ref[turn * per_turn + p, :rows, :],
                 slots_ref[turn * per_turn + p + 1, :rows, :], p // 2 * LANES)
        tall, wide = three_products(sketches[...])
        for left in range(0, width, 2 * BLOCK):
            right = left + 2 * BLOCK
            work[left:width, left:right] += dot(tall[left:, :], wide[left:right, :], NT, None)

    mine = mine_ref[:rows, :]
    fill(mine, mine, 0)
    own = solved.shape[0]
    work[width:, :] = sketches[:, :LANES].T[:own, :]
    live = jnp.sum(slots_ref[:, rows:rows + 1, :])
    eliminate(width, queries_ref, scores_ref, work, solved, live)


def gathered_scores(block, slots, queries, in_width, out_width):
    width = in_width * out_width
    own = block.shape[1] // TOKENS
    vmem = pl.BlockSpec(memory_space=pltpu.VMEM)
    return pl.pallas_call(
        functools.partial(whole_kernel, in_width, out_width),
        out_shape=jax.ShapeDtypeStruct((own, queries.shape[0]), jnp.float32),
        in_specs=[vmem] * 3,
        out_specs=vmem,
        scratch_shapes=[
            pltpu.VMEM((width + own, width), jnp.float32),
            pltpu.VMEM((own, width), jnp.float32),
            pltpu.VMEM((width, 2 * LANES), jnp.float32),
        ],
        compiler_params=pltpu.CompilerParams(vmem_limit_bytes=48 * 2**20),
        name="gathered_scores",
    )(block, slots, queries)


def on_device(sizes, hidden_acts, out_grads, loss_mask, proj_in, proj_out, queries):
    dp_size, query_size = sizes
    seq_count, seq_tokens, hidden_width = hidden_acts.shape
    in_width, out_width = proj_in.shape[0], proj_out.shape[0]
    gathered = lax.all_gather(queries, "query", axis=0, tiled=True)
    is_live = loss_mask.astype(jnp.float32)
    doubling = dp_size & (dp_size - 1) == 0 and dp_size >= 8 and query_size == 2
    if (doubling and dp_size * query_size <= MOST_GATHERED and seq_tokens == TOKENS
            and seq_count == LANES // 2):
        project = functools.partial(
            lax.dot_general, dimension_numbers=(((1,), (2,)), ((), ())),
            preferred_element_type=jnp.float32)
        live = is_live.T[None]
        acts = project(proj_in, hidden_acts).transpose(0, 2, 1)
        grads = project(proj_out, out_grads).transpose(0, 2, 1) * live
        packed = jnp.concatenate(
            [grads, acts, jnp.broadcast_to(live, (SUB, *live.shape[1:]))], axis=0)
        block = packed.reshape(in_width + out_width + SUB, seq_tokens * seq_count)
        slots = gather_blocks(block, dp_size).reshape(-1, *block.shape)
        return gathered_scores(block, slots, gathered, in_width, out_width)
    tokens = (seq_count * seq_tokens, -1)
    project = functools.partial(
        lax.dot_general, dimension_numbers=(((1,), (1,)), ((), ())),
        preferred_element_type=jnp.float32)
    act_proj = project(hidden_acts.reshape(tokens), proj_in)
    grad_proj = project(out_grads.reshape(tokens), proj_out)
    act_proj = act_proj.reshape(seq_count, seq_tokens, in_width)
    weighted = grad_proj.reshape(seq_count, seq_tokens, out_width) * is_live[:, :, None]
    outer = jnp.einsum("stg,stx->sgx", weighted, act_proj, precision=HIGHEST)
    sketch = outer.reshape(seq_count, -1) / lax.psum(jnp.sum(is_live), NAMES)
    gram = lax.dot_general(sketch, sketch, (((0,), (0,)), ((), ())), precision=HIGHEST)
    return solve_scores(lax.psum(gram, NAMES), sketch, gathered)


def solution(mesh):
    return jax.shard_map(
        functools.partial(on_device, (mesh.shape["dp"], mesh.shape["query"])),
        mesh=mesh,
        in_specs=(
            P(("dp", "query"), None, None),
            P(("dp", "query"), None, None),
            P(("dp", "query"), None),
            P(),
            P(),
            P("query", None),
        ),
        out_specs=P(("dp", "query"), None),
        check_vma=False,
    )
```

```python
import functools

import jax
import jax.numpy as jnp
from jax import lax
from jax.experimental import pallas as pl
from jax.experimental.pallas import tpu as pltpu
from jax.sharding import PartitionSpec as P

BLOCK = 128
SUB = 8
LANES = 128
TOKENS = 4
MOST_GATHERED = 64
HIGHEST = lax.Precision.HIGHEST
NN = (((1,), (0,)), ((), ()))
NT = (((1,), (1,)), ((), ()))


def dot(a, b, dims=NN, precision=HIGHEST):
    return lax.dot_general(a, b, dims, precision=precision, preferred_element_type=jnp.float32)


def halves_of(x):
    high = x.astype(jnp.bfloat16)
    return high, (x - high.astype(jnp.float32)).astype(jnp.bfloat16)


def three_products(x, y=None):
    x_high, x_low = halves_of(x)
    y_high, y_low = (x_high, x_low) if y is None else halves_of(y)
    return (jnp.concatenate([x_high, x_high, x_low], axis=1),
            jnp.concatenate([y_high, y_low, y_high], axis=1))


def dot3(x, y):
    x_high, x_low = halves_of(x)
    y_high, y_low = halves_of(y)
    return dot(jnp.concatenate([x_high, x_high, x_low], axis=1),
               jnp.concatenate([y_high, y_low, y_high], axis=0), NN, None)


def negated_inverse(block):
    size = block.shape[0]
    tiles = size // SUB
    rows = [block[SUB * t:SUB * (t + 1), :] for t in range(tiles)]
    lane = lax.broadcasted_iota(jnp.int32, (SUB, size), 1)
    sub = lax.broadcasted_iota(jnp.int32, (SUB, size), 0)

    def spread(x, at):
        return jnp.broadcast_to(x[:, at:at + 1], (SUB, size))

    def across(x, at):
        return jnp.broadcast_to(x[at:at + 1, :], (SUB, size))

    for t in range(tiles):
        first = SUB * t
        inside = (lane >= first) & (lane < first + SUB)
        columns = [spread(rows[t], first + i) for i in range(SUB)]
        panel = jnp.where(inside, jnp.where(lane - first == sub, -1.0, 0.0), rows[t])
        for i in range(0, SUB, 2):
            p, q = columns[i], columns[i + 1]
            a, b, c = across(p, i), across(p, i + 1), across(q, i + 1)
            inverse = 1.0 / (a * c - b * b)
            at_first, at_second = sub == i, sub == i + 1

            def eliminate_pair(x):
                u, v = across(x, i), across(x, i + 1)
                first_row = (c * u - b * v) * inverse
                second_row = (a * v - b * u) * inverse
                rest = (x - p * first_row) - q * second_row
                return jnp.where(at_first, first_row, jnp.where(at_second, second_row, rest))

            panel = eliminate_pair(panel)
            for j in range(i + 2, SUB):
                columns[j] = eliminate_pair(columns[j])
        spread_panel = [across(panel, i) for i in range(SUB)]
        updated = []
        for u in range(tiles):
            if u == t:
                updated.append(panel)
                continue
            terms = [spread(rows[u], first + i) * spread_panel[i] for i in range(SUB)]
            while len(terms) > 1:
                terms = [terms[i] + terms[i + 1] for i in range(0, len(terms), 2)]
            updated.append(jnp.where(inside, 0.0, rows[u]) - terms[0])
        rows = updated
    return jnp.concatenate(rows, axis=0)


def solve_kernel(fisher_ref, sketch_ref, queries_ref, scores_ref, work, solved):
    width = fisher_ref.shape[0]
    work[:width, :] = fisher_ref[...]
    work[width:, :] = sketch_ref[...]
    eliminate(width, queries_ref, scores_ref, work, solved, 1.0)


def eliminate(width, queries_ref, scores_ref, work, solved, factor):
    blocks = width // BLOCK
    diagonal = (lax.broadcasted_iota(jnp.int32, (BLOCK, BLOCK), 0)
                == lax.broadcasted_iota(jnp.int32, (BLOCK, BLOCK), 1))
    spans = [pl.ds(b * BLOCK, BLOCK) for b in range(blocks)]
    kept = jnp.zeros((BLOCK, BLOCK), jnp.float32)
    for span in spans:
        kept = kept + jnp.where(diagonal, work[span, span], 0.0)
    damping = jnp.full((BLOCK, BLOCK), 0.1 * jnp.sum(kept) / width)
    per_damping = 1.0 / damping

    @pl.loop(0, blocks)
    def _(k):
        start = pl.multiple_of(k * BLOCK, BLOCK)
        here = pl.ds(start, BLOCK)
        block = work[here, here]
        scaled_block = block * per_damping
        inverse = -per_damping * negated_inverse(
            jnp.where(diagonal, scaled_block + 1.0, scaled_block))
        for b in range(blocks):
            @pl.when(k == b)
            def _():
                below = (b + 1) * BLOCK
                panel = work[below:, spans[b]]
                scaled = dot3(panel, inverse)
                work[below:, spans[b]] = scaled
                if below == width:
                    return
                tall, wide = three_products(scaled, panel[:width - below, :])
                for left in range(below, width, 2 * BLOCK):
                    right = min(left + 2 * BLOCK, width)
                    work[left:, left:right] -= dot(
                        tall[left - below:, :], wide[left - below:right - below, :], NT, None)

    solved[:, spans[-1]] = work[width:, spans[-1]]
    for b in range(blocks - 2, -1, -1):
        above = (b + 1) * BLOCK
        solved[:, spans[b]] = work[width:, spans[b]] - dot3(
            solved[:, above:], work[above:width, spans[b]])
    tall, wide = three_products(solved[...], queries_ref[...])
    scores_ref[...] = dot(tall, wide, NT, None) * factor


def solve_scores(fisher, sketch, queries):
    width = fisher.shape[0]
    rows = sketch.shape[0]
    whole = pl.BlockSpec(memory_space=pltpu.VMEM)
    return pl.pallas_call(
        solve_kernel,
        out_shape=jax.ShapeDtypeStruct((rows, queries.shape[0]), jnp.float32),
        in_specs=[whole] * 3,
        out_specs=whole,
        scratch_shapes=[
            pltpu.VMEM((width + rows, width), jnp.float32),
            pltpu.VMEM((rows, width), jnp.float32),
        ],
        compiler_params=pltpu.CompilerParams(vmem_limit_bytes=48 * 2**20),
        name="solve_scores",
    )(fisher, sketch, queries)


NAMES = ("dp", "query")


def gather_kernel(dims, mine_ref, slots_ref, own_sem, send_sem, recv_sem):
    n = len(dims)
    dp, core = lax.axis_index("dp"), lax.axis_index("query")
    bits = [lax.rem(lax.div(dp, d), 2) for d in dims]
    partners = [dp + d - 2 * d * bit for d, bit in zip(dims, bits)]
    everyone = [{"dp": p, "query": core} for p in partners] + [{"dp": dp, "query": 1 - core}]

    barrier = pltpu.get_barrier_semaphore()
    for device in everyone:
        pl.semaphore_signal(barrier, inc=1, device_id=device, device_id_type=pl.DeviceIdType.MESH)
    own = pltpu.make_async_copy(mine_ref, slots_ref.at[(core, *bits)], own_sem)
    own.start()
    own.wait()
    pl.semaphore_wait(barrier, len(everyone))

    count = [0]
    copies = []

    def send(index, device):
        part = slots_ref.at[index]
        at = count[0]
        count[0] += 1
        copy = pltpu.make_async_remote_copy(
            src_ref=part, dst_ref=part, send_sem=send_sem.at[at], recv_sem=recv_sem.at[at],
            device_id=device, device_id_type=pl.DeviceIdType.MESH)
        copy.start()
        copies.append(copy)
        return copy

    def forward(index):
        return send(index, everyone[-1])

    every = slice(None)
    siblings = [forward((core, *bits))]
    held = list(bits)
    for a in range(n - 2):
        send((core, *held), everyone[a]).wait_recv()
        came = list(held)
        came[a] = 1 - bits[a]
        siblings.append(forward((core, *came)))
        held[a] = every
    halves = [(0, (n - 2, n - 1)), (1, (n - 1, n - 2))]
    helds = []
    for half, _ in halves:
        one = list(held)
        one[0] = half
        helds.append(one)
    for turn in range(2):
        flying = [send((core, *helds[h]), everyone[order[turn]]) for h, order in halves]
        for (h, order), copy in zip(halves, flying):
            copy.wait_recv()
            axis = order[turn]
            came = list(helds[h])
            came[axis] = 1 - bits[axis]
            siblings.append(forward((core, *came)))
            helds[h][axis] = every
    for copy in siblings:
        copy.wait_recv()
    for copy in copies:
        copy.wait_send()


def gather_blocks(block, dp_size):
    dims = []
    d = dp_size // 2
    while d:
        dims.append(d)
        d //= 2
    n = len(dims)
    transfers = 2 * (n - 2 + 4) + 1
    anywhere = pl.BlockSpec(memory_space=pl.ANY)
    return pl.pallas_call(
        functools.partial(gather_kernel, tuple(dims)),
        out_shape=jax.ShapeDtypeStruct((2,) + (2,) * n + block.shape, block.dtype),
        in_specs=[anywhere],
        out_specs=anywhere,
        scratch_shapes=[
            pltpu.SemaphoreType.DMA,
            pltpu.SemaphoreType.DMA((transfers,)),
            pltpu.SemaphoreType.DMA((transfers,)),
        ],
        compiler_params=pltpu.CompilerParams(collective_id=0, has_side_effects=True),
        name="gather_tokens",
    )(block)


def pair_sketch(first, second, in_width, out_width):
    lanes = 2 * LANES
    low = lax.broadcasted_iota(jnp.int32, (in_width + out_width, LANES), 1) < LANES // 2
    total = None
    for start in range(0, lanes, LANES):
        one, two = first[:, start:start + LANES], second[:, start:start + LANES]
        for token in (jnp.where(low, one, pltpu.roll(two, LANES // 2, 1)),
                      jnp.where(low, pltpu.roll(one, LANES // 2, 1), two)):
            acts = token[out_width:, :]
            term = [token[g:g + 1, :] * acts for g in range(out_width)]
            total = term if total is None else [t + u for t, u in zip(total, term)]
    return total


def whole_kernel(in_width, out_width, mine_ref, slots_hbm, queries_hbm, scores_ref,
                 work, solved, sketches, slots_ref, queries_ref, slot_sems, query_sem):
    width = in_width * out_width
    rows = in_width + out_width
    devices = slots_ref.shape[0]
    per_turn = sketches.shape[1] // (LANES // 2)

    def fill(first, second, column):
        parts = pair_sketch(first, second, in_width, out_width)
        for g, part in enumerate(parts):
            sketches[g * in_width:(g + 1) * in_width, column:column + LANES] = part

    def slot_copy(turn):
        part = pl.ds(turn * per_turn, per_turn)
        return pltpu.make_async_copy(slots_hbm.at[part], slots_ref.at[part], slot_sems.at[turn])

    for turn in range(devices // per_turn):
        slot_copy(turn).start()
    query_copy = pltpu.make_async_copy(queries_hbm, queries_ref, query_sem)
    query_copy.start()
    work[:width, :] = jnp.zeros((width, width), jnp.float32)

    @pl.loop(0, devices // per_turn)
    def _(turn):
        slot_copy(turn).wait()
        for p in range(0, per_turn, 2):
            fill(slots_ref[turn * per_turn + p, :rows, :],
                 slots_ref[turn * per_turn + p + 1, :rows, :], p // 2 * LANES)
        tall, wide = three_products(sketches[...])
        for left in range(0, width, 2 * BLOCK):
            right = left + 2 * BLOCK
            work[left:width, left:right] += dot(tall[left:, :], wide[left:right, :], NT, None)

    mine = mine_ref[:rows, :]
    fill(mine, mine, 0)
    own = solved.shape[0]
    work[width:, :] = sketches[:, :LANES].T[:own, :]
    live = jnp.sum(slots_ref[:, rows:rows + 1, :])
    query_copy.wait()
    eliminate(width, queries_ref, scores_ref, work, solved, live)


def gathered_scores(block, slots, queries, in_width, out_width):
    width = in_width * out_width
    own = block.shape[1] // TOKENS
    per_turn = 4
    vmem = pl.BlockSpec(memory_space=pltpu.VMEM)
    return pl.pallas_call(
        functools.partial(whole_kernel, in_width, out_width),
        out_shape=jax.ShapeDtypeStruct((own, queries.shape[0]), jnp.float32),
        in_specs=[vmem, pl.BlockSpec(memory_space=pl.ANY), pl.BlockSpec(memory_space=pl.ANY)],
        out_specs=vmem,
        scratch_shapes=[
            pltpu.VMEM((width + own, width), jnp.float32),
            pltpu.VMEM((own, width), jnp.float32),
            pltpu.VMEM((width, per_turn * LANES // 2), jnp.float32),
            pltpu.VMEM(slots.shape, jnp.float32),
            pltpu.VMEM(queries.shape, jnp.float32),
            pltpu.SemaphoreType.DMA((slots.shape[0] // per_turn,)),
            pltpu.SemaphoreType.DMA,
        ],
        compiler_params=pltpu.CompilerParams(vmem_limit_bytes=48 * 2**20),
        name="gathered_scores",
    )(block, slots, queries)


def on_device(sizes, hidden_acts, out_grads, loss_mask, proj_in, proj_out, queries):
    dp_size, query_size = sizes
    seq_count, seq_tokens, hidden_width = hidden_acts.shape
    in_width, out_width = proj_in.shape[0], proj_out.shape[0]
    gathered = lax.all_gather(queries, "query", axis=0, tiled=True)
    is_live = loss_mask.astype(jnp.float32)
    doubling = dp_size & (dp_size - 1) == 0 and dp_size >= 8 and query_size == 2
    if (doubling and dp_size * query_size <= MOST_GATHERED and seq_tokens == TOKENS
            and seq_count == LANES // 2):
        project = functools.partial(
            lax.dot_general, dimension_numbers=(((1,), (2,)), ((), ())),
            preferred_element_type=jnp.float32)
        live = is_live.T[None]
        acts = project(proj_in, hidden_acts).transpose(0, 2, 1)
        grads = project(proj_out, out_grads).transpose(0, 2, 1) * live
        packed = jnp.concatenate(
            [grads, acts, jnp.broadcast_to(live, (SUB, *live.shape[1:]))], axis=0)
        block = packed.reshape(in_width + out_width + SUB, seq_tokens * seq_count)
        slots = gather_blocks(block, dp_size).reshape(-1, *block.shape)
        return gathered_scores(block, slots, gathered, in_width, out_width)
    tokens = (seq_count * seq_tokens, -1)
    project = functools.partial(
        lax.dot_general, dimension_numbers=(((1,), (1,)), ((), ())),
        preferred_element_type=jnp.float32)
    act_proj = project(hidden_acts.reshape(tokens), proj_in)
    grad_proj = project(out_grads.reshape(tokens), proj_out)
    act_proj = act_proj.reshape(seq_count, seq_tokens, in_width)
    weighted = grad_proj.reshape(seq_count, seq_tokens, out_width) * is_live[:, :, None]
    outer = jnp.einsum("stg,stx->sgx", weighted, act_proj, precision=HIGHEST)
    sketch = outer.reshape(seq_count, -1) / lax.psum(jnp.sum(is_live), NAMES)
    gram = lax.dot_general(sketch, sketch, (((0,), (0,)), ((), ())), precision=HIGHEST)
    return solve_scores(lax.psum(gram, NAMES), sketch, gathered)


def solution(mesh):
    return jax.shard_map(
        functools.partial(on_device, (mesh.shape["dp"], mesh.shape["query"])),
        mesh=mesh,
        in_specs=(
            P(("dp", "query"), None, None),
            P(("dp", "query"), None, None),
            P(("dp", "query"), None),
            P(),
            P(),
            P("query", None),
        ),
        out_specs=P(("dp", "query"), None),
        check_vma=False,
    )
```
